32 devices in a mesh: mem: 4 (over x, core), lev: 8 (over z, y).
Axes of the slice: x: 2, y: 2, z: 4, core: 2. Of those that a mesh axis runs over, the one named last changes fastest.
Arguments:
- alpha_weights: float32 [4, 16, 384, 512], P('mem', 'lev'), may hold values from -6 to 6
- perturbations: bfloat16 [4, 16, 393216], P('mem', None, 'lev'), may hold values from -6 to 6
- coef_x: float32 [384, 512], replicated, may hold values from 0.02 to 0.24
- coef_y: float32 [384, 512], replicated, may hold values from 0.02 to 0.24
- level_scale: float32 [16], replicated, may hold values from 0.3 to 1
- level_map: int32 [16], replicated, may hold values from 0 to 15, each once
- tile_widths: int32 [8], replicated, may hold values from 1 to 49152, 196608 in all
- band_widths: int32 [16], replicated, may hold values from 1 to 4, as said below
Outputs:
- increment: float32 [16, 393216], P('mem', 'lev')
The draws below stay inside these ranges and needn't reach their ends.
Inputs may be any that keep to these rules, and one draw needn't show every extreme that they name: `level_map`: a permutation of the levels. `tile_widths`: sum to 196608; the largest equals 49152. `band_widths`: some level has a band of exactly 4.
All inputs are finite; a program needn't handle non-finite values.
Results may differ from the reference program's by a relative error of at most 0.0035.
Values may be sent and summed in bfloat16 or wider, within the bound.
A program may use at most 64 MiB of HBM per device.

```python
import math
import jax
import jax.numpy as jnp
import numpy as np
from jax import lax

NX = 384
NY = 512
STEPS = 16
BAND = 4
NLEV = 16
MEMBERS = 4
TILES = 8
CAP = 49152


def draw_band_widths(key, part):
    spot_key, fill_key = jax.random.split(jax.random.fold_in(key, 7))
    widths_drawn = jax.random.randint(fill_key, (NLEV,), 1, BAND + 1)
    marked = jax.random.randint(spot_key, (), 0, NLEV)
    return jnp.where(jnp.arange(NLEV) == marked, BAND, widths_drawn).astype(jnp.int32)


def spiked(entries, stream_key, source, target, blocks, factor):
    def block_of(dim):
        return (jnp.arange(entries.shape[dim]) // (entries.shape[dim] // blocks)).reshape((-1,) + (1,) * (entries.ndim - 1 - dim))

    one_side = jax.random.permutation(stream_key, blocks)[block_of(target)]
    far = (block_of(target) + blocks // 2) % blocks
    return jnp.where((block_of(source) == one_side) | (block_of(source) == far), factor * entries, entries)


def level_of(key, extent, pieces, low, largest):
    def one(axis_at, shards_of):
        heights = jax.random.uniform(jax.random.fold_in(jax.random.fold_in(key, 6), axis_at), (shards_of,), jnp.float32, low / len(pieces), largest / len(pieces))
        return jnp.repeat(jnp.exp(heights), extent[axis_at] // shards_of).reshape((-1,) + (1,) * (len(extent) - axis_at - 1))

    level = one(*pieces[0])
    for cut in pieces[1:]:
        level = level * one(*cut)
    return level


def length_profile(number_of, total, reach, skew):
    loads = [(1 << 20) // math.isqrt(grade ** skew) + 1 for grade in range(2, number_of + 1)]
    spare, holding = total - reach - (number_of - 1), [1] * (number_of - 1)
    while spare > 0:
        candidates = [i for i in range(number_of - 1) if holding[i] < reach]
        pool, left = sum([loads[i] for i in candidates]), spare
        for i in candidates:
            extra = min(reach - holding[i], max(1, left * loads[i] // pool), spare)
            holding[i] = holding[i] + extra
            spare = spare - extra
    return np.array([reach] + holding)


def ragged_sizes(stream_key, number_of, total, limit, skew):
    if number_of == 2:
        one = jax.random.randint(stream_key, (), max(1, total - limit), min(limit, total - 1) + 1)
        return jnp.stack([one, total - one])
    sizes = jnp.asarray(length_profile(number_of, total, limit, skew), jnp.int32)
    twos = (number_of - 1) // 2
    donor, taker = sizes[1:1 + 2 * twos:2], sizes[2:2 + 2 * twos:2]
    slack = jnp.minimum(donor - 1, limit - taker)
    moved = jax.random.randint(jax.random.fold_in(stream_key, 1), (twos,), 0, 1 << 20) % (slack + 1)
    sizes = sizes.at[1:1 + 2 * twos:2].set(donor - moved).at[2:2 + 2 * twos:2].set(taker + moved)
    return sizes[jax.random.permutation(jax.random.fold_in(stream_key, 2), number_of)]


def bell_draw(stream_key, shape, width, most, cuts=(), kind=jnp.bfloat16):
    result = jax.random.normal(stream_key, shape, jnp.float32) * width
    if len(cuts) > 0:
        result = level_of(stream_key, shape, cuts, -0.22, 0.18) * result
    return jnp.clip(result, min=-most, max=most).astype(kind)


def bell_draw_with(stream_key, dims, scale, most, shards, heavy, kind=jnp.bfloat16):
    array = scale * jax.random.normal(stream_key, dims, jnp.float32)
    if shards:
        array = array * level_of(stream_key, dims, shards, -0.22, 0.18)
    return jnp.clip(spiked(array, jax.random.fold_in(stream_key, 3), *heavy), -most, most).astype(kind)


def setup_inputs(seed: int = 0) -> dict:
    keys = jax.random.split(jax.random.key(seed), 9)
    return {
        "alpha_weights": bell_draw(keys[0], (MEMBERS, NLEV, NX, NY), 1.0, 6.0, ((0, 4), (1, 8)), jnp.float32),
        "perturbations": bell_draw_with(keys[1], (MEMBERS, NLEV, TILES * CAP), 1.0, 6.0, ((0, 4), (2, 8)), (0, 1, 4, 2.0)),
        "coef_x": jnp.clip(jax.random.uniform(keys[2], (NX, NY), jnp.float32, 0.02, 0.24), 0.02, 0.24),
        "coef_y": jnp.clip(jax.random.uniform(keys[3], (NX, NY), jnp.float32, 0.02, 0.24), 0.02, 0.24),
        "level_scale": jnp.clip(jnp.exp(jax.random.uniform(keys[4], (NLEV,), jnp.float32, math.log(0.3), math.log(1.0))), 0.3, 1.0),
        "level_map": jax.random.permutation(keys[5], NLEV).astype(jnp.int32),
        "tile_widths": ragged_sizes(keys[6], TILES, NX * NY, CAP, 2).astype(jnp.int32),
        "band_widths": draw_band_widths(jax.random.fold_in(keys[8], 71), 0),
    }


def diffuse_level(layer_field, scaled_x, scaled_y):
    def step_once(index_step, state):
        flux_x = scaled_x[:-1, :] * (state[1:, :] - state[:-1, :])
        flux_y = scaled_y[:, :-1] * (state[:, 1:] - state[:, :-1])
        zero_row = jnp.zeros((1, state.shape[1]), state.dtype)
        zero_col = jnp.zeros((state.shape[0], 1), state.dtype)
        change = jnp.concatenate([flux_x, zero_row], 0) - jnp.concatenate([zero_row, flux_x], 0)
        change = change + jnp.concatenate([flux_y, zero_col], 1) - jnp.concatenate([zero_col, flux_y], 1)
        return state + change
    return lax.fori_loop(0, STEPS, step_once, layer_field)


def vertical_matrix(band_widths):
    level_pos = jnp.arange(band_widths.shape[0])
    distance = jnp.abs(level_pos[:, None] - level_pos[None, :]).astype(jnp.float32)
    mutual = jnp.minimum(band_widths[:, None], band_widths[None, :]).astype(jnp.float32)
    return jnp.where(distance <= mutual, jnp.exp(-distance * distance / (mutual * mutual)), 0.0)


def reference(alpha_weights, perturbations, coef_x, coef_y, level_scale, level_map, tile_widths, band_widths):
    starts = jnp.cumsum(tile_widths) - tile_widths
    slot_pos = jnp.arange(TILES * CAP)
    tile_id = slot_pos // CAP
    offset = slot_pos % CAP
    valid_cols = offset < tile_widths[tile_id]
    column = jnp.minimum(starts[tile_id] + offset, NX * NY - 1).astype(jnp.int32)
    localizer = vertical_matrix(band_widths).astype(jnp.bfloat16)
    slot_scale = level_scale[level_map]

    def smooth_slot(member_field, strength):
        return diffuse_level(member_field, coef_x * strength, coef_y * strength)

    def member(running, member_pair):
        member_field, pert_rows = member_pair
        smooth = jax.vmap(smooth_slot)(member_field, slot_scale)
        rounded = smooth.astype(jnp.bfloat16).reshape(NLEV, NX * NY)
        physical = jnp.zeros_like(rounded).at[level_map].set(rounded)
        tiled_cols = physical[:, column]
        spread = jnp.dot(localizer, tiled_cols, preferred_element_type=jnp.float32)
        return running + jnp.where(valid_cols[None, :], pert_rows.astype(jnp.float32) * spread, 0.0), None

    running, unused = lax.scan(member, jnp.zeros((NLEV, TILES * CAP), jnp.float32), (alpha_weights, perturbations))
    return running
```

```python
import functools

import jax
import jax.numpy as jnp
from jax import lax
from jax.experimental import pallas as pl
from jax.experimental.pallas import tpu as pltpu
from jax.sharding import PartitionSpec as P

STEPS = 16
SUB = 8
LANES = 128
ROWS = 16
MESH = pl.DeviceIdType.MESH


def smooth_kernel(
    scale_ref, map_ref, width_ref, alpha_ref, cx_ref, cy_ref, out_ref, state, gx, gy,
    flat, flat_x, flat_y,
):
    lev_dev, nx, ny = alpha_ref.shape[1:]
    tiles = out_ref.shape[0]
    nr, nq = nx // SUB, ny // LANES
    first_slot = lax.axis_index("lev") * lev_dev
    sub = lax.broadcasted_iota(jnp.int32, (SUB, ny), 0)
    col = lax.broadcasted_iota(jnp.int32, (SUB, ny), 1)
    lane = lax.broadcasted_iota(jnp.int32, (ROWS, LANES), 1)

    for slot in range(lev_dev):
        gain = scale_ref[map_ref[first_slot + slot]]

        def spread_rows(ref, into):
            def block(i, carry):
                rows = pl.ds(pl.multiple_of(i * SUB, SUB), SUB)
                for q in range(nq):
                    into[pl.ds(i * SUB * nq + q, SUB, stride=nq), :] = ref[
                        rows, q * LANES : (q + 1) * LANES
                    ]
                return carry

            lax.fori_loop(0, nr, block, 0, unroll=2)

        spread_rows(alpha_ref.at[0, slot], flat)
        if slot == 0:
            spread_rows(cx_ref, flat_x)
            spread_rows(cy_ref, flat_y)

        def stage(r, carry):
            for q in range(nq):
                here = slice(q * LANES, (q + 1) * LANES)
                rows = pl.ds(r * nq + q, SUB, stride=nr * nq)
                state[r, :, here] = flat[rows, :]
                gx[r, :, here] = flat_x[rows, :] * gain
                gy[r, :, here] = flat_y[rows, :] * gain
            gy[r] = jnp.where(col < ny - 1, gy[r], 0.0)
            return carry

        lax.fori_loop(0, nr, stage, 0)
        gx[nr - 1] = jnp.where(sub < SUB - 1, gx[nr - 1], 0.0)

        def step(_, carry):
            top = state[0]
            beyond = pltpu.roll(top, SUB - 1, 0)
            last_flux = gx[nr - 1] * (beyond - state[nr - 1])

            def update(r, cur, above, flux_before):
                flux_x = gx[r] * (above - cur)
                flux_y = gy[r] * (pltpu.roll(cur, ny - 1, 1) - cur)
                state[r] = cur + ((flux_x - flux_before) + (flux_y - pltpu.roll(flux_y, 1, 1)))
                return above, flux_x

            def row(r, rc):
                return update(r, rc[0], state[r + 1], rc[1])

            cur, flux = lax.fori_loop(
                0, nr - 1, row, (top, pltpu.roll(last_flux, 1, 0)), unroll=4
            )
            update(nr - 1, cur, beyond, flux)
            return carry

        lax.fori_loop(0, STEPS, step, 0)

        def flatten(r, carry):
            for q in range(nq):
                flat[pl.ds(r * nq + q, SUB, stride=nr * nq), :] = state[
                    r, :, q * LANES : (q + 1) * LANES
                ]
            return carry

        lax.fori_loop(0, nr, flatten, 0)

        start = jnp.int32(0)
        for tile in range(tiles):
            width = width_ref[tile]
            row0, shift = start // LANES, start % LANES
            turn = lax.rem(LANES - shift, LANES)
            keep = lane < LANES - shift

            def cut(n, carry, row0=row0, turn=turn, keep=keep, tile=tile):
                low = pltpu.roll(flat[pl.ds(row0 + n * ROWS, ROWS), :], turn, 1)
                high = pltpu.roll(flat[pl.ds(row0 + n * ROWS + 1, ROWS), :], turn, 1)
                out_ref[tile, slot, pl.ds(pl.multiple_of(n * ROWS, ROWS), ROWS), :] = jnp.where(
                    keep, low, high
                ).astype(jnp.bfloat16)
                return carry

            per = ROWS * LANES
            lax.fori_loop(0, (width + per - 1) // per, cut, 0)
            start = start + width


def merge_kernel(
    n_mem, n_lev, chunks,
    map_ref, width_ref, band_ref, tiles_ref, pert_ref, out_ref,
    pert_buf, arr, send_buf, recv_buf, own, pert_t, weight, tmp, tmp_out,
    a_send, a_recv, b_send, b_recv, p_sem, o_sem,
):
    lev_dev, rows_all = tiles_ref.shape[1:3]
    levels = pert_ref.shape[1]
    share = levels // n_mem
    rows_c = rows_all // chunks
    groups = rows_c // ROWS
    me_mem, me_lev = lax.axis_index("mem"), lax.axis_index("lev")

    pert_copy = pltpu.make_async_copy(pert_ref.at[0], pert_buf, p_sem)
    pert_copy.start()
    barrier = pltpu.get_barrier_semaphore()
    for p in range(1, n_lev):
        pl.semaphore_signal(
            barrier, inc=1, device_id=(me_mem, lax.rem(me_lev + p, n_lev)), device_id_type=MESH
        )
    for o in range(1, n_mem):
        pl.semaphore_signal(
            barrier, inc=1, device_id=(lax.rem(me_mem + o, n_mem), me_lev), device_id_type=MESH
        )
    pl.semaphore_wait(barrier, n_lev + n_mem - 2)

    def tile_copy(c, p):
        to = lax.rem(me_lev + p, n_lev)
        rows = pl.ds(pl.multiple_of(c * rows_c, ROWS), rows_c)
        return pltpu.make_async_remote_copy(
            src_ref=tiles_ref.at[to, :, rows, :],
            dst_ref=arr.at[c, p],
            send_sem=a_send.at[c, p],
            recv_sem=a_recv.at[c, p],
            device_id=(me_mem, to),
            device_id_type=MESH,
        )

    def own_copy(c):
        rows = pl.ds(pl.multiple_of(c * rows_c, ROWS), rows_c)
        return pltpu.make_async_copy(tiles_ref.at[me_lev, :, rows, :], arr.at[c, 0], o_sem.at[c])

    def sum_copy(c, o):
        return pltpu.make_async_remote_copy(
            src_ref=send_buf.at[c, o - 1],
            dst_ref=recv_buf.at[c, o - 1],
            send_sem=b_send.at[c, o - 1],
            recv_sem=b_recv.at[c, o - 1],
            device_id=(lax.rem(me_mem + o, n_mem), me_lev),
            device_id_type=MESH,
        )

    def send_all(c, carry):
        own_copy(c).start()
        for p in range(1, n_lev):
            tile_copy(c, p).start()
        return carry

    lax.fori_loop(0, chunks, send_all, 0)

    def weigh(n, carry):
        p, rest = n // levels, lax.rem(n, levels)
        dest = lax.rem(me_mem + rest // share, n_mem)
        k = dest * share + lax.rem(rest, share)
        src = lax.rem(me_lev - p + n_lev, n_lev)
        for slot in range(lev_dev):
            level = map_ref[src * lev_dev + slot]
            d = jnp.abs(jnp.full((SUB, LANES), k - level, jnp.int32)).astype(jnp.float32)
            b = jnp.full((SUB, LANES), jnp.minimum(band_ref[k], band_ref[level]), jnp.int32)
            b = b.astype(jnp.float32)
            value = jnp.where(d <= b, jnp.exp(-d * d / (b * b)), 0.0)
            weight[rest, p * lev_dev + slot] = value.astype(jnp.bfloat16).astype(jnp.float32)
        return carry

    lax.fori_loop(0, n_lev * levels, weigh, 0)

    pert_copy.wait()

    def turn(g, carry):
        for cb in range(ROWS):
            at = pl.multiple_of((g * ROWS + cb) * LANES, LANES)
            tmp[cb * levels : (cb + 1) * levels, :] = pert_buf[:, pl.ds(at, LANES)].astype(
                jnp.float32
            )
        rows = pl.ds(pl.multiple_of(g * ROWS, ROWS), ROWS)
        for k in range(levels):
            pert_t[k, rows, :] = tmp[pl.ds(k, ROWS, stride=levels), :]
        return carry

    lax.fori_loop(0, rows_all // ROWS, turn, 0)

    width = width_ref[me_lev]
    place = lax.broadcasted_iota(jnp.int32, (ROWS, LANES), 0) * LANES + lax.broadcasted_iota(
        jnp.int32, (ROWS, LANES), 1
    )

    def finish(c):
        for o in range(1, n_mem):
            sum_copy(c, o).wait_recv()

        def add(g, carry):
            rows = pl.ds(pl.multiple_of(g * ROWS, ROWS), ROWS)
            first = c * rows_c + g * ROWS
            for kk in range(share):
                total = own[kk, pl.ds(pl.multiple_of(first, ROWS), ROWS), :]
                for o in range(1, n_mem):
                    total = total + recv_buf[c, o - 1, kk, rows, :].astype(jnp.float32)
                tmp_out[pl.ds(kk, ROWS, stride=share), :] = total
            for cb in range(ROWS):
                at = pl.multiple_of((first + cb) * LANES, LANES)
                out_ref[:, pl.ds(at, LANES)] = tmp_out[cb * share : (cb + 1) * share, :]
            return carry

        lax.fori_loop(0, groups, add, 0)

    def chunk(c, carry):
        own_copy(c).wait()
        for p in range(1, n_lev):
            tile_copy(c, p).wait_recv()

        def group(g, inner):
            rows = pl.ds(pl.multiple_of(g * ROWS, ROWS), ROWS)
            first = c * rows_c + g * ROWS
            rows_at = pl.ds(pl.multiple_of(first, ROWS), ROWS)
            valid = place < width - first * LANES
            held = [
                [
                    arr[c, s // lev_dev, s % lev_dev, rows, :].astype(jnp.float32)[
                        h * SUB : (h + 1) * SUB
                    ]
                    for h in range(ROWS // SUB)
                ]
                for s in range(levels)
            ]
            for o in range(n_mem):
                dest = lax.rem(me_mem + o, n_mem)
                for kk in range(share):
                    sums = [None] * (ROWS // SUB)
                    for s in range(levels):
                        w = weight[o * share + kk, s]
                        for h in range(ROWS // SUB):
                            term = w * held[s][h]
                            sums[h] = term if s == 0 else sums[h] + term
                    spread = jnp.concatenate(sums, 0)
                    value = jnp.where(
                        valid, pert_t[dest * share + kk, rows_at, :] * spread, 0.0
                    )
                    if o == 0:
                        own[kk, rows_at, :] = value
                    else:
                        send_buf[c, o - 1, kk, rows, :] = value.astype(jnp.bfloat16)
            return inner

        lax.fori_loop(0, groups, group, 0)
        for o in range(1, n_mem):
            sum_copy(c, o).start()
        return carry

    chunk(0, 0)

    def chunk_and_finish(c, carry):
        chunk(c, 0)
        finish(c - 1)
        return carry

    lax.fori_loop(1, chunks, chunk_and_finish, 0)
    finish(chunks - 1)

    def drain(c, carry):
        for p in range(1, n_lev):
            tile_copy(c, p).wait_send()
        for o in range(1, n_mem):
            sum_copy(c, o).wait_send()
        return carry

    lax.fori_loop(0, chunks, drain, 0)


def body(
    n_mem, n_lev,
    alpha_weights, perturbations, coef_x, coef_y, level_scale, level_map, tile_widths, band_widths,
):
    lev_dev, nx, ny = alpha_weights.shape[1:]
    levels, cap = perturbations.shape[1:]
    rows_all = cap // LANES
    share = levels // n_mem
    chunks = 4
    rows_c = rows_all // chunks
    smem = pl.BlockSpec(memory_space=pltpu.SMEM)
    vmem = pl.BlockSpec(memory_space=pltpu.VMEM)
    anywhere = pl.BlockSpec(memory_space=pl.ANY)
    nr, flat_rows = nx // SUB, nx * ny // LANES

    tiles = pl.pallas_call(
        smooth_kernel,
        out_shape=jax.ShapeDtypeStruct((n_lev, lev_dev, rows_all, LANES), jnp.bfloat16),
        in_specs=[smem] * 3 + [vmem] * 3,
        out_specs=vmem,
        scratch_shapes=[
            pltpu.VMEM((nr, SUB, ny), jnp.float32),
            pltpu.VMEM((nr, SUB, ny), jnp.float32),
            pltpu.VMEM((nr, SUB, ny), jnp.float32),
            pltpu.VMEM((flat_rows + 2 * ROWS, LANES), jnp.float32),
            pltpu.VMEM((flat_rows, LANES), jnp.float32),
            pltpu.VMEM((flat_rows, LANES), jnp.float32),
        ],
        compiler_params=pltpu.CompilerParams(vmem_limit_bytes=40 << 20),
        name="smooth",
    )(level_scale, level_map, tile_widths, alpha_weights, coef_x, coef_y)

    return pl.pallas_call(
        functools.partial(merge_kernel, n_mem, n_lev, chunks),
        out_shape=jax.ShapeDtypeStruct((share, cap), jnp.float32),
        in_specs=[smem] * 3 + [anywhere] * 2,
        out_specs=vmem,
        scratch_shapes=[
            pltpu.VMEM((levels, cap), jnp.bfloat16),
            pltpu.VMEM((chunks, n_lev, lev_dev, rows_c, LANES), jnp.bfloat16),
            pltpu.VMEM((chunks, n_mem - 1, share, rows_c, LANES), jnp.bfloat16),
            pltpu.VMEM((chunks, n_mem - 1, share, rows_c, LANES), jnp.bfloat16),
            pltpu.VMEM((share, rows_all, LANES), jnp.float32),
            pltpu.VMEM((levels, rows_all, LANES), jnp.float32),
            pltpu.VMEM((levels, levels, SUB, LANES), jnp.float32),
            pltpu.VMEM((ROWS * levels, LANES), jnp.float32),
            pltpu.VMEM((ROWS * share, LANES), jnp.float32),
            pltpu.SemaphoreType.DMA((chunks, n_lev)),
            pltpu.SemaphoreType.DMA((chunks, n_lev)),
            pltpu.SemaphoreType.DMA((chunks, n_mem - 1)),
            pltpu.SemaphoreType.DMA((chunks, n_mem - 1)),
            pltpu.SemaphoreType.DMA,
            pltpu.SemaphoreType.DMA((chunks,)),
        ],
        compiler_params=pltpu.CompilerParams(
            collective_id=0, has_side_effects=True, vmem_limit_bytes=40 << 20
        ),
        name="merge",
    )(level_map, tile_widths, band_widths, tiles, perturbations)


def solution(mesh):
    placed = (P("mem", "lev", None, None), P("mem", None, "lev"), P(), P(), P(), P(), P(), P())

    return jax.shard_map(
        functools.partial(body, mesh.shape["mem"], mesh.shape["lev"]),
        mesh=mesh,
        in_specs=placed,
        out_specs=P("mem", "lev"),
        check_vma=False,
    )
```

```python
import functools

import jax
import jax.numpy as jnp
from jax import lax
from jax.experimental import pallas as pl
from jax.experimental.pallas import tpu as pltpu
from jax.sharding import PartitionSpec as P

STEPS = 16
SUB = 8
LANES = 128
ROWS = 16
MESH = pl.DeviceIdType.MESH


def largest_divisor(n, most):
    return next(d for d in range(min(n, most), 0, -1) if n % d == 0)


def smooth_kernel(
    scale_ref, map_ref, width_ref, alpha_hbm, cx_hbm, cy_hbm, out_ref,
    alpha, cx, cy, ping, pong, gx, gy, flat, flat_x, flat_y, sem,
):
    lev_dev, nx, ny = alpha.shape
    tiles, rows_all = out_ref.shape[0], out_ref.shape[2]
    nr, nq = nx // SUB, ny // LANES
    pitch = nr * nq + 1
    per_trip = largest_divisor(nr, 24)
    cut_rows = largest_divisor(rows_all // ROWS, 8) * ROWS
    first_slot = lax.axis_index("lev") * lev_dev
    sub = lax.broadcasted_iota(jnp.int32, (SUB, ny), 0)
    lane8 = lax.broadcasted_iota(jnp.int32, (SUB, LANES), 1)
    lane = lax.broadcasted_iota(jnp.int32, (ROWS, LANES), 1)

    copies = [
        pltpu.make_async_copy(cx_hbm, cx, sem.at[0]),
        pltpu.make_async_copy(cy_hbm, cy, sem.at[1]),
    ] + [
        pltpu.make_async_copy(alpha_hbm.at[0, slot], alpha.at[slot], sem.at[2 + slot])
        for slot in range(lev_dev)
    ]
    for copy in copies:
        copy.start()

    at_i = lax.broadcasted_iota(jnp.int32, (ny, ny), 0)
    at_j = lax.broadcasted_iota(jnp.int32, (ny, ny), 1)
    mix = (at_i == (at_j % LANES) * nq + at_j // LANES).astype(jnp.bfloat16)
    unmix = (at_j == (at_i % LANES) * nq + at_i // LANES).astype(jnp.bfloat16)

    def next_column(x):
        return jnp.concatenate([x[:, LANES:], pltpu.roll(x[:, :LANES], LANES - 1, 1)], 1)

    def column_before(x):
        return jnp.concatenate([pltpu.roll(x[:, -LANES:], 1, 1), x[:, :-LANES]], 1)

    def spread_rows(ref, into):
        x = ref[...]
        high = x.astype(jnp.bfloat16)
        rest = x - high.astype(jnp.float32)
        middle = rest.astype(jnp.bfloat16)
        low = (rest - middle.astype(jnp.float32)).astype(jnp.bfloat16)
        high, middle, low = (
            jnp.dot(part, mix, preferred_element_type=jnp.float32) for part in (high, middle, low)
        )
        mixed = (high + middle) + low
        for i in range(nx // SUB):
            for q in range(nq):
                into[pl.ds(i * SUB * nq + q + i * SUB // nr, SUB, stride=nq), :] = mixed[
                    i * SUB : (i + 1) * SUB, q * LANES : (q + 1) * LANES
                ]

    copies[0].wait()
    spread_rows(cx, flat_x)
    copies[1].wait()
    spread_rows(cy, flat_y)
    for slot in range(lev_dev):
        copies[2 + slot].wait()

    def level(slot, carry):
        gain = scale_ref[map_ref[first_slot + slot]]
        spread_rows(alpha.at[slot], flat)

        def stage(r, inner):
            for q in range(nq):
                here = slice(q * LANES, (q + 1) * LANES)
                rows = pl.ds(r * nq + q, SUB, stride=pitch)
                ping[r, :, here] = flat[rows, :]
                gx[r, :, here] = flat_x[rows, :] * gain
                face_y = flat_y[rows, :] * gain
                if q == nq - 1:
                    face_y = jnp.where(lane8 < LANES - 1, face_y, 0.0)
                gy[r, :, here] = face_y
            return inner

        lax.fori_loop(0, nr, stage, 0, unroll=largest_divisor(nr, 4))
        gx[nr - 1] = jnp.where(sub < SUB - 1, gx[nr - 1], 0.0)

        def step(src, dst):
            top = src[0]
            beyond = pltpu.roll(top, SUB - 1, 0)
            last_flux = gx[nr - 1] * (beyond - src[nr - 1])

            def sweep(base, count, cur, flux_before):
                for u in range(count):
                    r = base + u
                    above = beyond if isinstance(r, int) and r == nr - 1 else src[r + 1]
                    flux_x = gx[r] * (above - cur)
                    flux_y = gy[r] * (next_column(cur) - cur)
                    dst[r] = cur + ((flux_x - flux_before) + (flux_y - column_before(flux_y)))
                    cur, flux_before = above, flux_x
                return cur, flux_before

            state = lax.fori_loop(
                0,
                nr // per_trip - 1,
                lambda i, c: sweep(i * per_trip, per_trip, *c),
                (top, pltpu.roll(last_flux, 1, 0)),
            )
            sweep(nr - per_trip, per_trip, *state)

        def two_steps(_, inner):
            step(ping, pong)
            step(pong, ping)
            return inner

        lax.fori_loop(0, STEPS // 2, two_steps, 0)

        rounded = ping[...].reshape(nx, ny).astype(jnp.bfloat16)
        plain = jnp.dot(rounded, unmix, preferred_element_type=jnp.float32)
        for r in range(nr):
            for q in range(nq):
                flat[pl.ds(r * nq + q, SUB, stride=nr * nq), :] = plain[
                    r * SUB : (r + 1) * SUB, q * LANES : (q + 1) * LANES
                ]

        def cut_tile(tile, start):
            width = width_ref[tile]
            row0, shift = start // LANES, start % LANES
            turn = lax.rem(LANES - shift, LANES)
            keep = lane < LANES - shift

            def cut(n, inner):
                for h in range(cut_rows // ROWS):
                    at = n * cut_rows + h * ROWS
                    low = pltpu.roll(flat[pl.ds(row0 + at, ROWS), :], turn, 1)
                    high = pltpu.roll(flat[pl.ds(row0 + at + 1, ROWS), :], turn, 1)
                    out_ref[tile, slot, pl.ds(pl.multiple_of(at, ROWS), ROWS), :] = jnp.where(
                        keep, low, high
                    ).astype(jnp.bfloat16)
                return inner

            per = cut_rows * LANES
            lax.fori_loop(0, (width + per - 1) // per, cut, 0)
            return start + width

        lax.fori_loop(0, tiles, cut_tile, jnp.int32(0))
        return carry

    lax.fori_loop(0, lev_dev, level, 0)


def merge_kernel(
    n_mem, n_lev, chunks,
    map_ref, width_ref, band_ref, tiles_ref, pert_ref, out_ref,
    pert_buf, arr, send_buf, recv_buf, own, pert_t, weight, tmp, tmp_out,
    a_send, a_recv, b_send, b_recv, p_sem, o_sem,
):
    lev_dev, rows_all = tiles_ref.shape[1:3]
    levels = pert_ref.shape[1]
    share = levels // n_mem
    rows_c = rows_all // chunks
    groups = rows_c // ROWS
    me_mem, me_lev = lax.axis_index("mem"), lax.axis_index("lev")

    pert_copy = pltpu.make_async_copy(pert_ref.at[0], pert_buf, p_sem)
    pert_copy.start()
    barrier = pltpu.get_barrier_semaphore()
    for p in range(1, n_lev):
        pl.semaphore_signal(
            barrier, inc=1, device_id=(me_mem, lax.rem(me_lev + p, n_lev)), device_id_type=MESH
        )
    for o in range(1, n_mem):
        pl.semaphore_signal(
            barrier, inc=1, device_id=(lax.rem(me_mem + o, n_mem), me_lev), device_id_type=MESH
        )
    pl.semaphore_wait(barrier, n_lev + n_mem - 2)

    def tile_copy(c, p):
        to = lax.rem(me_lev + p, n_lev)
        rows = pl.ds(pl.multiple_of(c * rows_c, ROWS), rows_c)
        return pltpu.make_async_remote_copy(
            src_ref=tiles_ref.at[to, :, rows, :],
            dst_ref=arr.at[c, p],
            send_sem=a_send.at[c, p],
            recv_sem=a_recv.at[c, p],
            device_id=(me_mem, to),
            device_id_type=MESH,
        )

    def own_copy(c):
        rows = pl.ds(pl.multiple_of(c * rows_c, ROWS), rows_c)
        return pltpu.make_async_copy(tiles_ref.at[me_lev, :, rows, :], arr.at[c, 0], o_sem.at[c])

    def sum_copy(c, o):
        return pltpu.make_async_remote_copy(
            src_ref=send_buf.at[c, o - 1],
            dst_ref=recv_buf.at[c, o - 1],
            send_sem=b_send.at[c, o - 1],
            recv_sem=b_recv.at[c, o - 1],
            device_id=(lax.rem(me_mem + o, n_mem), me_lev),
            device_id_type=MESH,
        )

    def send_all(c, carry):
        own_copy(c).start()
        for p in range(1, n_lev):
            tile_copy(c, p).start()
        return carry

    lax.fori_loop(0, chunks, send_all, 0)

    def weigh(n, carry):
        p, rest = n // levels, lax.rem(n, levels)
        dest = lax.rem(me_mem + rest // share, n_mem)
        k = dest * share + lax.rem(rest, share)
        src = lax.rem(me_lev - p + n_lev, n_lev)
        for slot in range(lev_dev):
            level = map_ref[src * lev_dev + slot]
            d = jnp.abs(jnp.full((SUB, LANES), k - level, jnp.int32)).astype(jnp.float32)
            b = jnp.full((SUB, LANES), jnp.minimum(band_ref[k], band_ref[level]), jnp.int32)
            b = b.astype(jnp.float32)
            value = jnp.where(d <= b, jnp.exp(-d * d / (b * b)), 0.0)
            weight[rest, p * lev_dev + slot] = value.astype(jnp.bfloat16).astype(jnp.float32)
        return carry

    lax.fori_loop(0, n_lev * levels, weigh, 0)

    pert_copy.wait()

    def turn(g, carry):
        for cb in range(ROWS):
            at = pl.multiple_of((g * ROWS + cb) * LANES, LANES)
            tmp[cb * levels : (cb + 1) * levels, :] = pert_buf[:, pl.ds(at, LANES)].astype(
                jnp.float32
            )
        rows = pl.ds(pl.multiple_of(g * ROWS, ROWS), ROWS)
        for k in range(levels):
            pert_t[k, rows, :] = tmp[pl.ds(k, ROWS, stride=levels), :]
        return carry

    lax.fori_loop(0, rows_all // ROWS, turn, 0)

    width = width_ref[me_lev]
    place = lax.broadcasted_iota(jnp.int32, (ROWS, LANES), 0) * LANES + lax.broadcasted_iota(
        jnp.int32, (ROWS, LANES), 1
    )

    def finish(c):
        for o in range(1, n_mem):
            sum_copy(c, o).wait_recv()

        def add(g, carry):
            rows = pl.ds(pl.multiple_of(g * ROWS, ROWS), ROWS)
            first = c * rows_c + g * ROWS
            for kk in range(share):
                total = own[kk, pl.ds(pl.multiple_of(first, ROWS), ROWS), :]
                for o in range(1, n_mem):
                    total = total + recv_buf[c, o - 1, kk, rows, :].astype(jnp.float32)
                tmp_out[pl.ds(kk, ROWS, stride=share), :] = total
            for cb in range(ROWS):
                at = pl.multiple_of((first + cb) * LANES, LANES)
                out_ref[:, pl.ds(at, LANES)] = tmp_out[cb * share : (cb + 1) * share, :]
            return carry

        lax.fori_loop(0, groups, add, 0)

    def chunk(c, carry):
        own_copy(c).wait()
        for p in range(1, n_lev):
            tile_copy(c, p).wait_recv()

        def group(g, inner):
            rows = pl.ds(pl.multiple_of(g * ROWS, ROWS), ROWS)
            first = c * rows_c + g * ROWS
            rows_at = pl.ds(pl.multiple_of(first, ROWS), ROWS)
            valid = place < width - first * LANES
            held = [
                [
                    arr[c, s // lev_dev, s % lev_dev, rows, :].astype(jnp.float32)[
                        h * SUB : (h + 1) * SUB
                    ]
                    for h in range(ROWS // SUB)
                ]
                for s in range(levels)
            ]
            for o in range(n_mem):
                dest = lax.rem(me_mem + o, n_mem)
                for kk in range(share):
                    sums = [None] * (ROWS // SUB)
                    for s in range(levels):
                        w = weight[o * share + kk, s]
                        for h in range(ROWS // SUB):
                            term = w * held[s][h]
                            sums[h] = term if s == 0 else sums[h] + term
                    spread = jnp.concatenate(sums, 0)
                    value = jnp.where(
                        valid, pert_t[dest * share + kk, rows_at, :] * spread, 0.0
                    )
                    if o == 0:
                        own[kk, rows_at, :] = value
                    else:
                        send_buf[c, o - 1, kk, rows, :] = value.astype(jnp.bfloat16)
            return inner

        lax.fori_loop(0, groups, group, 0)
        for o in range(1, n_mem):
            sum_copy(c, o).start()
        return carry

    chunk(0, 0)

    def chunk_and_finish(c, carry):
        chunk(c, 0)
        finish(c - 1)
        return carry

    lax.fori_loop(1, chunks, chunk_and_finish, 0)
    finish(chunks - 1)

    def drain(c, carry):
        for p in range(1, n_lev):
            tile_copy(c, p).wait_send()
        for o in range(1, n_mem):
            sum_copy(c, o).wait_send()
        return carry

    lax.fori_loop(0, chunks, drain, 0)


def body(
    n_mem, n_lev,
    alpha_weights, perturbations, coef_x, coef_y, level_scale, level_map, tile_widths, band_widths,
):
    lev_dev, nx, ny = alpha_weights.shape[1:]
    levels, cap = perturbations.shape[1:]
    rows_all = cap // LANES
    share = levels // n_mem
    chunks = 4
    rows_c = rows_all // chunks
    smem = pl.BlockSpec(memory_space=pltpu.SMEM)
    vmem = pl.BlockSpec(memory_space=pltpu.VMEM)
    anywhere = pl.BlockSpec(memory_space=pl.ANY)
    nr, flat_rows = nx // SUB, nx * ny // LANES

    grid = [pltpu.VMEM((nr, SUB, ny), jnp.float32)] * 4
    tiles = pl.pallas_call(
        smooth_kernel,
        out_shape=jax.ShapeDtypeStruct((n_lev, lev_dev, rows_all, LANES), jnp.bfloat16),
        in_specs=[smem] * 3 + [anywhere] * 3,
        out_specs=vmem,
        scratch_shapes=[
            pltpu.VMEM((lev_dev, nx, ny), jnp.float32),
            pltpu.VMEM((nx, ny), jnp.float32),
            pltpu.VMEM((nx, ny), jnp.float32),
            *grid,
            pltpu.VMEM((flat_rows + 10 * ROWS, LANES), jnp.float32),
            pltpu.VMEM((flat_rows + SUB, LANES), jnp.float32),
            pltpu.VMEM((flat_rows + SUB, LANES), jnp.float32),
            pltpu.SemaphoreType.DMA((2 + lev_dev,)),
        ],
        compiler_params=pltpu.CompilerParams(vmem_limit_bytes=58 << 20),
        name="smooth",
    )(level_scale, level_map, tile_widths, alpha_weights, coef_x, coef_y)

    return pl.pallas_call(
        functools.partial(merge_kernel, n_mem, n_lev, chunks),
        out_shape=jax.ShapeDtypeStruct((share, cap), jnp.float32),
        in_specs=[smem] * 3 + [anywhere] * 2,
        out_specs=vmem,
        scratch_shapes=[
            pltpu.VMEM((levels, cap), jnp.bfloat16),
            pltpu.VMEM((chunks, n_lev, lev_dev, rows_c, LANES), jnp.bfloat16),
            pltpu.VMEM((chunks, n_mem - 1, share, rows_c, LANES), jnp.bfloat16),
            pltpu.VMEM((chunks, n_mem - 1, share, rows_c, LANES), jnp.bfloat16),
            pltpu.VMEM((share, rows_all, LANES), jnp.float32),
            pltpu.VMEM((levels, rows_all, LANES), jnp.float32),
            pltpu.VMEM((levels, levels, SUB, LANES), jnp.float32),
            pltpu.VMEM((ROWS * levels, LANES), jnp.float32),
            pltpu.VMEM((ROWS * share, LANES), jnp.float32),
            pltpu.SemaphoreType.DMA((chunks, n_lev)),
            pltpu.SemaphoreType.DMA((chunks, n_lev)),
            pltpu.SemaphoreType.DMA((chunks, n_mem - 1)),
            pltpu.SemaphoreType.DMA((chunks, n_mem - 1)),
            pltpu.SemaphoreType.DMA,
            pltpu.SemaphoreType.DMA((chunks,)),
        ],
        compiler_params=pltpu.CompilerParams(
            collective_id=0, has_side_effects=True, vmem_limit_bytes=58 << 20
        ),
        name="merge",
    )(level_map, tile_widths, band_widths, tiles, perturbations)


def solution(mesh):
    placed = (P("mem", "lev", None, None), P("mem", None, "lev"), P(), P(), P(), P(), P(), P())

    return jax.shard_map(
        functools.partial(body, mesh.shape["mem"], mesh.shape["lev"]),
        mesh=mesh,
        in_specs=placed,
        out_specs=P("mem", "lev"),
        check_vma=False,
    )
```
